256 devices in a mesh: row: 8 (over y, core), col: 32 (over x, z).
Axes of the slice: x: 4, y: 4, z: 8, core: 2. Of those that a mesh axis runs over, the one named last changes fastest.
Arguments:
- amplitudes: float32 [8192, 4096], P('row', 'col'), may hold values from -6 to 6
- integrals: float32 [4096, 16384], P(None, 'col'), may hold values from -0.125 to 0.125
- screen: int32 [32, 128], P(None, 'col'), may hold values 0 or 1
- slab_order: int32 [32], replicated, may hold values from 0 to 31, each once
- weights: float32 [8192, 16384], P('row', 'col'), may hold values from 0.05 to 1
Outputs:
- ladder: float32 [8192, 16384], P('row', 'col')
- energy: float32 [], replicated
The draws below stay inside these ranges and needn't reach their ends.
Inputs may be any that keep to these rules, and one draw needn't show every extreme that they name: `slab_order`: each of 0 to 31 appears once.
All inputs are finite; a program needn't handle non-finite values. No bound on the sum of `screen` on one device may be relied on, other than what follows from the above.
Results may differ from the reference program's by a relative error of at most 0.00007.
Values sent between devices are 32-bit elements; how exact they have to be, the bound alone decides.
No kernel may reach another device: no remote copies, remote signals or barrier semaphores. Data moves between devices by JAX's collectives and lax.ppermute only.
A program may use at most 128 MiB of HBM per device.

```python
import math
import jax
import jax.numpy as jnp
from jax import lax

B = 128
KT = 32
K = 4096
NT = 128
AB = 16384
IJ = 8192


def place_ends(values, stream_key, low, high):
    shape = values.shape
    index_at = [jax.random.randint(jax.random.fold_in(stream_key, axis), (), 0, shape[axis]) for axis in range(len(shape))]
    values = values.at[tuple(index_at)].set(low)
    longest = shape.index(max(shape))
    index_at[longest] = (index_at[longest] + 1) % shape[longest]
    return values.at[tuple(index_at)].set(high)


def level_of(own_key, dims, cuts, smallest, top_value):
    gain = 1.0
    for axis_at, blocks in cuts:
        steps = jax.random.uniform(jax.random.fold_in(jax.random.fold_in(own_key, 6), axis_at), (blocks,), jnp.float32, smallest / len(cuts), top_value / len(cuts))
        gain = gain * jnp.repeat(jnp.exp(steps), dims[axis_at] // blocks).reshape((-1,) + (1,) * (len(dims) - 1 - axis_at))
    return gain


def noise(key, shape, spread, bound, split=(), dtype=jnp.bfloat16):
    gain = level_of(key, shape, split, -0.22, 0.18) if split else 1.0
    array = jax.random.normal(key, shape, jnp.float32) * spread * gain
    return jnp.minimum(jnp.maximum(array, -bound), bound).astype(dtype)


def setup_inputs(seed: int = 0) -> dict:
    seeds = jax.random.split(jax.random.key(seed), 6)
    return {
        "amplitudes": noise(seeds[0], (IJ, K), 1.0, 6.0, ((0, 8), (1, 32)), jnp.float32),
        "integrals": noise(seeds[1], (K, AB), (K // 2) ** -0.5, 0.125, ((1, 32),), jnp.float32),
        "screen": place_ends((jax.random.randint(seeds[2], (KT, NT), 0, 2) < 1).astype(jnp.int32), jax.random.fold_in(seeds[2], 1), 0, 1),
        "slab_order": jax.random.permutation(seeds[3], KT).astype(jnp.int32),
        "weights": jnp.clip(jnp.exp(math.log(1.0) - 2.9957323 * jax.random.uniform(seeds[4], (IJ, AB), jnp.float32) ** level_of(seeds[4], (IJ, AB), ((0, 8), (1, 32)), -0.2, 0.2)), 0.05, 1.0),
    }


def reference(amplitudes, integrals, screen, slab_order, weights):
    factor = screen.astype(jnp.float32)[:, None, :, None]
    masked = (integrals.reshape(KT, B, NT, B) * factor).reshape(KT, B, AB)
    placed = jnp.take(masked, slab_order, axis=0).reshape(K, AB)
    ladder = 0.5 * jnp.dot(amplitudes, placed, precision=lax.Precision.HIGHEST, preferred_element_type=jnp.float32)
    energy = jnp.sum(weights * ladder * ladder) / (IJ * AB)
    return ladder, energy
```

```python
import functools

import jax
import jax.numpy as jnp
from jax import lax
from jax.experimental import pallas as pl
from jax.experimental.pallas import tpu as pltpu
from jax.sharding import PartitionSpec as P

NX, NZ = 4, 8
XPOS = (0, -1, 1, 2)
ZPOS = (0, -1, 1, -2, 2, -3, 3, 4)
T = 128
MIB = 2**20


def shift(v, axis, d):
    pairs = []
    for row in range(lax.axis_size("row")):
        step = d if row % 2 == 0 else -d
        for x in range(NX):
            for z in range(NZ):
                to = (x + step) % NX * NZ + z if axis == "x" else x * NZ + (z + step) % NZ
                pairs.append((row * NX * NZ + x * NZ + z, row * NX * NZ + to))
    return lax.ppermute(v, ("row", "col"), pairs)


def top(v):
    return v[: v.shape[0] // 2]


def bottom(v):
    return v[v.shape[0] // 2 :]


class Line:
    def __init__(self):
        self.seen = ()

    def step(self, done, *values):
        values = lax.optimization_barrier(((*self.seen, *done), *values))[1:]
        self.seen = tuple(done)
        return values[0] if len(values) == 1 else values


def near(values):
    return [pltpu.with_memory_space_constraint(v, pltpu.VMEM) for v in values]


def whole(n):
    return [pl.BlockSpec(memory_space=pltpu.VMEM)] * n


def split(value):
    high = value.astype(jnp.bfloat16)
    return high, (value - high.astype(jnp.float32)).astype(jnp.bfloat16)


def prepare_kernel(order_ref, screen_ref, b_ref, high_ref, low_ref, slabs, arrived):
    count, _, width = slabs.shape

    def copy(i):
        source = b_ref.at[pl.ds(pl.multiple_of(order_ref[i] * T, T), T), :]
        return pltpu.make_async_copy(source, slabs.at[i], arrived.at[i])

    @pl.loop(0, count)
    def _(i):
        copy(i).start()

    @pl.loop(0, count)
    def _(i):
        copy(i).wait()
        rows = pl.ds(pl.multiple_of(i * T, T), T)
        for n in range(width // T):
            columns = pl.ds(n * T, T)
            kept = slabs[i, :, columns] * screen_ref[order_ref[i], n].astype(jnp.float32)
            high_ref[rows, columns], low_ref[rows, columns] = split(kept)


def prepare(order, screen, integrals):
    depth, width = integrals.shape
    return pl.pallas_call(
        prepare_kernel,
        out_shape=[pltpu.VMEM((depth, width), jnp.bfloat16)] * 2,
        in_specs=[pl.BlockSpec(memory_space=pltpu.SMEM)] * 2 + [pl.BlockSpec(memory_space=pltpu.HBM)],
        out_specs=whole(2),
        scratch_shapes=[pltpu.VMEM((depth // T, T, width), jnp.float32), pltpu.SemaphoreType.DMA((depth // T,))],
        compiler_params=pltpu.CompilerParams(vmem_limit_bytes=12 * MIB),
        name="prepare",
    )(order, screen, integrals)


def product(slabs, height, high_ref, low_ref):
    left = jnp.concatenate([piece[pl.ds(row, height), pl.ds(c * T, T)] for piece, row, c, place in slabs], axis=1)
    right = [jnp.concatenate([ref[pl.ds(s[3] * T, T), :] for s in slabs], axis=0) for ref in (high_ref, low_ref)]
    high, low = split(left)
    dot = functools.partial(jnp.dot, preferred_element_type=jnp.float32)
    two = dot(jnp.concatenate([high, low], axis=0), right[0])
    return two[:height] + (two[height:] + dot(high, right[1]))


def sums(blocks, work, pieces, high_ref, low_ref, emit):
    for (start, height), slabs in zip(blocks, work):
        slabs = [(pieces[i], row, c, place) for i, row, c, place in slabs]
        emit(start, height, product(slabs, height, high_ref, low_ref) if slabs else None)


def middle_kernel(blocks, work, n, first, *refs):
    pieces, (high_ref, low_ref), rest = refs[:n], refs[n : n + 2], refs[n + 2 :]
    total = rest[-1]

    def emit(start, height, value):
        rows = pl.ds(start, height)
        if value is not None:
            total[rows, :] = value if first else rest[0][rows, :] + value

    sums(blocks, work, pieces, high_ref, low_ref, emit)


def middle(blocks, pieces, work, high, low, totals):
    width = high.shape[1]
    n = len(pieces)
    return pl.pallas_call(
        functools.partial(middle_kernel, blocks, work, n, not totals),
        out_shape=pltpu.VMEM((sum(height for _, height in blocks), width), jnp.float32),
        in_specs=whole(n + 2 + len(totals)),
        out_specs=whole(1)[0],
        input_output_aliases={n + 2 + i: i for i in range(len(totals))},
        compiler_params=pltpu.CompilerParams(vmem_limit_bytes=20 * MIB),
        name="middle",
    )(*near((*pieces, high, low, *totals)))


def last_kernel(blocks, work, n, *refs):
    pieces, (high_ref, low_ref, total, weights_ref, ladder_ref, energy_ref) = refs[:n], refs[n:]
    energy_ref[...] = jnp.zeros_like(energy_ref)

    def emit(start, height, value):
        rows = pl.ds(start, height)
        value = 0.5 * (total[rows, :] + value)
        width = value.shape[1]
        ladder_ref[rows, :] = value
        terms = (weights_ref[rows, :] * value * value).reshape(height // 8, 8, width).sum(axis=0)
        energy_ref[...] += sum(terms[:, i * T : (i + 1) * T] for i in range(width // T))

    sums(blocks, work, pieces, high_ref, low_ref, emit)


def last(blocks, pieces, work, high, low, total, weights):
    n = len(pieces)
    return pl.pallas_call(
        functools.partial(last_kernel, blocks, work, n),
        out_shape=[jax.ShapeDtypeStruct(weights.shape, jnp.float32), pltpu.VMEM((8, T), jnp.float32)],
        in_specs=whole(n + 4),
        out_specs=whole(2),
        compiler_params=pltpu.CompilerParams(vmem_limit_bytes=24 * MIB),
        name="last",
    )(*near((*pieces, high, low, total, weights)))


class Work:
    def __init__(self, blocks):
        self.blocks, self.pieces, self.slabs = blocks, [], [[], [], [], []]

    def add(self, members, piece, places):
        if isinstance(piece, tuple):
            half = len(members) // 2
            self.add(members[:half], piece[0], places)
            self.add(members[half:], piece[1], places)
            return
        row = 0
        for block in members:
            self.slabs[block] += [(len(self.pieces), row, c, place) for c, place in enumerate(places)]
            row += self.blocks[block][1]
        self.pieces.append(piece)

    def run(self, high, low, totals):
        return middle(self.blocks, self.pieces, self.slabs, high, low, totals)


ALL, INNER, OUTER = (0, 1, 2, 3), (1, 2), (0, 3)


def at(xpos, zpos):
    return zpos * NX + xpos


def local(amplitudes, integrals, screen, slab_order, weights):
    count = amplitudes.shape[0]
    outer = count * 13 // 64
    inner = count // 2 - outer
    heights = (outer, inner, inner, outer)
    blocks = tuple((sum(heights[:i]), h) for i, h in enumerate(heights))
    join = functools.partial(jnp.concatenate, axis=1)
    stack = functools.partial(jnp.concatenate, axis=0)
    me = lax.axis_index("col")
    x, z = me // NZ, me % NZ
    way = 1 - 2 * (lax.axis_index("row") % 2)
    xs = (x + way * jnp.array(XPOS)) % NX
    zs = (z + way * jnp.array(ZPOS)) % NZ
    order = slab_order[(zs[:, None] + xs[None, :] * NZ).reshape(-1)]
    inner_rows = lambda v: v[outer : outer + 2 * inner]
    outer_rows = lambda v: stack([v[:outer], v[outer + 2 * inner :]])

    line = Line()
    step = line.step
    px, pz = (functools.partial(shift, axis="x"), functools.partial(shift, axis="z"))
    a0 = amplitudes
    a1p, z1p = px(a0, d=1), pz(a0, d=1)
    a1m, z1m = px(a0, d=-1), pz(a0, d=-1)
    high, low = prepare(order, screen, integrals)
    line.seen = (high, low)
    a2p = px(step((a1p,), top(a1p)), d=1)
    z2p = pz(step((z1p,), z1p), d=1)
    a2m = px(step((a1m,), bottom(a1m)), d=-1)
    z2m = pz(step((z1m,), z1m), d=-1)
    g1 = join([inner_rows(z1p), inner_rows(z1m)])
    g1p = px(step((a2p,), g1), d=1)
    r0 = join([outer_rows(a1p), outer_rows(a1m), stack([a2p[:outer], a2m[inner:]])])
    r0, g1 = step((z2p, a2m), r0, g1)
    r1p = pz(r0, d=1)
    g1m = px(g1, d=-1)

    work = Work(blocks)
    work.add(ALL, a0, [at(0, 0)])
    work.add(ALL, a1p, [at(1, 0)])
    work.add(ALL, a1m, [at(2, 0)])
    work.add(ALL, z1p, [at(0, 1)])
    work.add(ALL, z1m, [at(0, 2)])
    work.add(ALL, (a2p, a2m), [at(3, 0)])
    total = work.run(high, low, [])

    z3p = pz(step((z2m, total), z2p), d=1)
    g2 = join([inner_rows(z2p), inner_rows(z2m)])
    g2p = px(step((g1p,), g2), d=1)
    z3m = pz(step((r1p,), z2m), d=-1)
    g2m = px(step((g1m,), g2), d=-1)

    work = Work(blocks)
    work.add(ALL, z2p, [at(0, 3)])
    work.add(ALL, z2m, [at(0, 4)])
    work.add(OUTER, r1p, [at(x, 1) for x in (1, 2, 3)])
    work.add(INNER, g1p, [at(1, z) for z in (1, 2)])
    work.add(INNER, g1m, [at(2, z) for z in (1, 2)])
    total = work.run(high, low, [total])

    r1m = pz(step((z3p, total), r0), d=-1)
    g1hp = px(step((g2p,), top(g1p)), d=1)
    z4p = pz(step((z3m,), top(z3p)), d=1)
    g1hm = px(step((g2m,), bottom(g1m)), d=-1)

    work = Work(blocks)
    work.add(ALL, z3p, [at(0, 5)])
    work.add(ALL, z3m, [at(0, 6)])
    work.add(INNER, g2p, [at(1, z) for z in (3, 4)])
    work.add(INNER, g2m, [at(2, z) for z in (3, 4)])
    total = work.run(high, low, [total])

    g3 = join([inner_rows(z3p), inner_rows(z3m)])
    g3p = px(step((g1hp, total), g3), d=1)
    z4m = pz(step((r1m,), bottom(z3m)), d=-1)
    r2p = pz(step((z4p,), r1p), d=1)
    g3m = px(step((g1hm,), g3), d=-1)
    r2m = pz(step((z4m,), r1m), d=-1)

    work = Work(blocks)
    work.add(ALL, (z4p, z4m), [at(0, 7)])
    work.add(OUTER, r1m, [at(x, 2) for x in (1, 2, 3)])
    work.add(INNER, (g1hp, g1hm), [at(3, z) for z in (1, 2)])
    total = work.run(high, low, [total])

    g2hp = px(step((g3p, total), top(g2p)), d=1)
    r3p = pz(step((r2p,), r2p), d=1)
    g2hm = px(step((g3m,), bottom(g2m)), d=-1)
    r3m = pz(step((r2m,), r2m), d=-1)
    g4 = stack([z4p[outer:], z4m[:inner]])
    g4p = px(step((g2hp,), g4), d=1)
    g4m = px(step((g2hm,), g4), d=-1)

    work = Work(blocks)
    work.add(OUTER, r2p, [at(x, 3) for x in (1, 2, 3)])
    work.add(OUTER, r2m, [at(x, 4) for x in (1, 2, 3)])
    work.add(INNER, g3p, [at(1, z) for z in (5, 6)])
    work.add(INNER, g3m, [at(2, z) for z in (5, 6)])
    work.add(INNER, (g2hp, g2hm), [at(3, z) for z in (3, 4)])
    total = work.run(high, low, [total])

    r4p, g3hp = step((r3p, g4p, total), top(r3p), top(g3p))
    r4p, g3hp = pz(r4p, d=1), px(g3hp, d=1)
    g3hm = px(step((g4m,), bottom(g3m)), d=-1)
    r4m, g4hp = step((r3m, g3hp), bottom(r3m), top(g4p))
    r4m, g4hp = pz(r4m, d=-1), px(g4hp, d=1)
    g4hm = px(step((g3hm,), bottom(g4m)), d=-1)

    work = Work(blocks)
    work.add(OUTER, r3p, [at(x, 5) for x in (1, 2, 3)])
    work.add(OUTER, r3m, [at(x, 6) for x in (1, 2, 3)])
    work.add(INNER, g4p, [at(1, 7)])
    work.add(INNER, g4m, [at(2, 7)])
    work.add(INNER, (g3hp, g3hm), [at(3, z) for z in (5, 6)])
    total = work.run(high, low, [total])

    total, a, b, c, d = step((), total, r4p, r4m, g4hp, g4hm)
    work = Work(blocks)
    work.add(INNER, (c, d), [at(3, 7)])
    work.add(OUTER, (a, b), [at(x, 7) for x in (1, 2, 3)])
    ladder, energy = last(blocks, work.pieces, work.slabs, high, low, total, weights)
    for axis in ("row", "col"):
        size = lax.axis_size(axis)
        energy = lax.all_to_all(jnp.broadcast_to(energy, (size, 8, T)), axis, 0, 0).sum(axis=0)
    cells = count * lax.axis_size("row") * weights.shape[1] * lax.axis_size("col")
    return ladder, jnp.sum(energy) / cells


def solution(mesh):
    return jax.shard_map(
        local,
        mesh=mesh,
        in_specs=(P("row", "col"), P(None, "col"), P(None, "col"), P(), P("row", "col")),
        out_specs=(P("row", "col"), P()),
        check_vma=False,
    )
```

```python
import functools

import jax
import jax.numpy as jnp
from jax import lax
from jax.experimental import pallas as pl
from jax.experimental.pallas import tpu as pltpu
from jax.sharding import PartitionSpec as P

NX, NZ = 4, 8
XPOS = (0, -1, 1, 2)
ZPOS = (0, -1, 1, -2, 2, -3, 3, 4)
T = 128
MIB = 2**20
SLOTS = 16


def shift(v, axis, d):
    pairs = []
    for row in range(lax.axis_size("row")):
        step = d if row % 2 == 0 else -d
        for x in range(NX):
            for z in range(NZ):
                to = (x + step) % NX * NZ + z if axis == "x" else x * NZ + (z + step) % NZ
                pairs.append((row * NX * NZ + x * NZ + z, row * NX * NZ + to))
    return lax.ppermute(v, ("row", "col"), pairs)


def cost(flops):
    return pl.CostEstimate(flops=flops, bytes_accessed=0, transcendentals=0)


def tick_kernel(token_ref, out_ref):
    out_ref[...] = token_ref[...]


class Line:
    def __init__(self, token):
        self.token = token

    def tick(self, flops):
        self.token = pl.pallas_call(
            tick_kernel,
            out_shape=pltpu.VMEM(self.token.shape, self.token.dtype),
            in_specs=whole(1),
            out_specs=whole(1)[0],
            compiler_params=pltpu.CompilerParams(vmem_limit_bytes=MIB),
            cost_estimate=cost(flops),
            name="tick",
        )(*near((self.token,)))

    def hold(self, *values):
        self.token, *values = lax.optimization_barrier((self.token, *values))
        return values[0] if len(values) == 1 else values


def near(values):
    return [pltpu.with_memory_space_constraint(v, pltpu.VMEM) for v in values]


def whole(n):
    return [pl.BlockSpec(memory_space=pltpu.VMEM)] * n


def split(value):
    high = value.astype(jnp.bfloat16)
    return high, (value - high.astype(jnp.float32)).astype(jnp.bfloat16)


def pack_kernel(runs, *refs):
    out_ref, start = refs[-1], 0
    for i, first, end in runs:
        out_ref[pl.ds(start, end - first), :] = refs[i][pl.ds(first, end - first), :]
        start += end - first


def pack(runs):
    arrays = list({id(array): array for array, _, _ in runs}.values())
    places = {id(array): i for i, array in enumerate(arrays)}
    runs = [(places[id(array)], first, end) for array, first, end in runs]
    height = sum(end - first for _, first, end in runs)
    return pl.pallas_call(
        functools.partial(pack_kernel, runs),
        out_shape=pltpu.VMEM((height, T), jnp.float32),
        in_specs=whole(len(arrays)),
        out_specs=whole(1)[0],
        compiler_params=pltpu.CompilerParams(vmem_limit_bytes=MIB),
        cost_estimate=cost(1),
        name="pack",
    )(*near(arrays))


def prepare_kernel(order_ref, screen_ref, b_ref, high_ref, low_ref, slabs, arrived):
    slots, _, width = slabs.shape
    count = b_ref.shape[0] // T

    def copy(i):
        source = b_ref.at[pl.ds(pl.multiple_of(order_ref[i] * T, T), T), :]
        return pltpu.make_async_copy(source, slabs.at[i % slots], arrived.at[i % slots])

    @pl.loop(0, slots)
    def _(i):
        copy(i).start()

    @pl.loop(0, count)
    def _(i):
        copy(i).wait()
        rows = pl.ds(pl.multiple_of(i * T, T), T)
        for n in range(width // T):
            columns = pl.ds(n * T, T)
            kept = slabs[i % slots, :, columns] * screen_ref[order_ref[i], n].astype(jnp.float32)
            high_ref[rows, columns], low_ref[rows, columns] = split(kept)

        @pl.when(i + slots < count)
        def _():
            copy(i + slots).start()


def prepare(order, screen, integrals):
    depth, width = integrals.shape
    return pl.pallas_call(
        prepare_kernel,
        out_shape=[pltpu.VMEM((depth, width), jnp.bfloat16)] * 2,
        in_specs=[pl.BlockSpec(memory_space=pltpu.SMEM)] * 2 + [pl.BlockSpec(memory_space=pltpu.HBM)],
        out_specs=whole(2),
        scratch_shapes=[pltpu.VMEM((SLOTS, T, width), jnp.float32), pltpu.SemaphoreType.DMA((SLOTS,))],
        cost_estimate=cost(1),
        compiler_params=pltpu.CompilerParams(vmem_limit_bytes=6 * MIB),
        name="prepare",
    )(order, screen, pltpu.with_memory_space_constraint(integrals, pltpu.HBM))


def product(slabs, height, high_ref, low_ref):
    left = jnp.concatenate([piece[pl.ds(row, height), pl.ds(c * T, T)] for piece, row, c, place in slabs], axis=1)
    right = [jnp.concatenate([ref[pl.ds(s[3] * T, T), :] for s in slabs], axis=0) for ref in (high_ref, low_ref)]
    high, low = split(left)
    dot = functools.partial(jnp.dot, preferred_element_type=jnp.float32)
    two = dot(jnp.concatenate([high, low], axis=0), right[0])
    return two[:height] + (two[height:] + dot(high, right[1]))


def sums(blocks, work, pieces, high_ref, low_ref, emit):
    for (start, height), slabs in zip(blocks, work):
        slabs = [(pieces[i], row, c, place) for i, row, c, place in slabs]
        emit(start, height, product(slabs, height, high_ref, low_ref) if slabs else None)


def middle_kernel(blocks, work, n, first, *refs):
    pieces, (high_ref, low_ref), rest = refs[:n], refs[n : n + 2], refs[n + 2 :]
    total = rest[-1]

    def emit(start, height, value):
        rows = pl.ds(start, height)
        if value is not None:
            total[rows, :] = value if first else rest[0][rows, :] + value

    sums(blocks, work, pieces, high_ref, low_ref, emit)


def middle(blocks, pieces, work, high, low, totals, flops):
    width = high.shape[1]
    n = len(pieces)
    return pl.pallas_call(
        functools.partial(middle_kernel, blocks, work, n, not totals),
        out_shape=pltpu.VMEM((sum(height for _, height in blocks), width), jnp.float32),
        in_specs=whole(n + 2 + len(totals)),
        out_specs=whole(1)[0],
        input_output_aliases={n + 2 + i: i for i in range(len(totals))},
        compiler_params=pltpu.CompilerParams(vmem_limit_bytes=12 * MIB),
        cost_estimate=cost(flops),
        name="middle",
    )(*near((*pieces, high, low, *totals)))


def last_kernel(blocks, work, n, *refs):
    pieces, (high_ref, low_ref, total, weights_ref, zero_ref, ladder_ref, energy_ref) = refs[:n], refs[n:]
    energy_ref[...] = zero_ref[...]

    def emit(start, height, value):
        rows = pl.ds(start, height)
        value = 0.5 * (total[rows, :] if value is None else total[rows, :] + value)
        width = value.shape[1]
        ladder_ref[rows, :] = value
        terms = (weights_ref[rows, :] * value * value).reshape(height // 8, 8, width).sum(axis=0)
        energy_ref[...] += sum(terms[:, i * T : (i + 1) * T] for i in range(width // T))

    sums(blocks, work, pieces, high_ref, low_ref, emit)


def last(blocks, pieces, work, high, low, total, weights, zero):
    n = len(pieces)
    return pl.pallas_call(
        functools.partial(last_kernel, blocks, work, n),
        out_shape=[jax.ShapeDtypeStruct(weights.shape, jnp.float32), pltpu.VMEM((8, T), jnp.float32)],
        in_specs=whole(n + 5),
        out_specs=whole(2),
        compiler_params=pltpu.CompilerParams(vmem_limit_bytes=12 * MIB),
        name="last",
    )(*near((*pieces, high, low, total, weights, zero)))


ALL, INNER, OUTER, B0, B1, B2, B3 = (0, 1, 2, 3), (1, 2), (0, 3), (0,), (1,), (2,), (3,)
SENDS = {
    ("x", 1): (
        [(0, 0, ALL)],
        [(-1, 0, (0, 1)), (0, -1, INNER)],
        [(0, 1, INNER), (0, -2, INNER), (-1, -1, B1)],
        [(0, 2, INNER), (0, -3, INNER), (-1, 1, B1), (-1, -2, B1)],
        [(0, 3, INNER), (0, 4, B1), (-1, 2, B1), (-1, -3, B1)],
        [(0, 4, B2), (-1, 3, B1), (-1, 4, B1)],
    ),
    ("x", -1): (
        [(0, 0, ALL)],
        [(1, 0, (2, 3)), (0, -1, INNER), (0, 1, INNER)],
        [(0, -2, INNER), (0, 2, INNER), (1, -1, B2), (1, 1, B2)],
        [(0, -3, INNER), (0, 3, INNER), (1, -2, B2), (1, 2, B2)],
        [(0, 4, INNER), (1, -3, B2), (1, 3, B2)],
        [(1, 4, B2)],
    ),
    ("z", 1): (
        [(0, 0, ALL)],
        [(0, -1, ALL), (-1, 0, OUTER)],
        [(0, -2, ALL), (-1, -1, OUTER), (1, 0, OUTER), (2, 0, B0)],
        [(0, -3, (0, 1)), (-1, -2, OUTER), (1, -1, OUTER), (2, -1, B0), (2, 0, B3)],
        [(-1, -3, B0), (1, -2, OUTER), (2, -2, B0), (2, -1, B3)],
        [(1, -3, B0), (2, -3, B0), (2, -2, B3)],
    ),
    ("z", -1): (
        [(0, 0, ALL)],
        [(0, 1, ALL), (-1, 0, OUTER), (1, 0, OUTER)],
        [(0, 2, ALL), (-1, 1, OUTER), (1, 1, OUTER), (2, 0, OUTER)],
        [(0, 3, (2, 3)), (-1, 2, OUTER), (1, 2, OUTER), (2, 1, OUTER)],
        [(-1, 3, B3), (1, 3, B3), (2, 2, OUTER)],
        [(2, 3, B3)],
    ),
}


def wrap(value, size):
    return (value + size // 2 - 1) % size - size // 2 + 1


class Held:
    def __init__(self, blocks, own):
        self.blocks, self.where, self.fresh = blocks, {}, []
        self.put(own, [(0, 0, ALL)])

    def put(self, array, items):
        row = 0
        for dx, dz, members in items:
            for block in members:
                key = (wrap(dx, NX), wrap(dz, NZ), block)
                assert key not in self.where
                self.where[key] = (array, row)
                self.fresh.append(key)
                row += self.blocks[block][1]
        assert row == array.shape[0]

    def rows(self, items):
        runs = []
        for dx, dz, members in items:
            for block in members:
                array, row = self.where[dx, dz, block]
                height = self.blocks[block][1]
                if runs and runs[-1][0] is array and runs[-1][2] == row:
                    runs[-1][2] = row + height
                else:
                    runs.append([array, row, row + height])
        if len(runs) == 1:
            array, first, end = runs[0]
            return array if (first, end) == (0, array.shape[0]) else array[first:end]
        return pack(runs)

    def work(self):
        pieces, slabs = [], [[], [], [], []]
        for key in self.fresh:
            dx, dz, block = key
            array, row = self.where[key]
            number = [i for i, piece in enumerate(pieces) if piece is array]
            if not number:
                number = [len(pieces)]
                pieces.append(array)
            slabs[block].append((number[0], row, 0, ZPOS.index(dz) * NX + XPOS.index(dx)))
        self.fresh = []
        return pieces, slabs


def local(amplitudes, integrals, screen, slab_order, weights):
    count = amplitudes.shape[0]
    outer = count * 13 // 64
    inner = count // 2 - outer
    heights = (outer, inner, inner, outer)
    blocks = tuple((sum(heights[:i]), h) for i, h in enumerate(heights))
    me = lax.axis_index("col")
    x, z = me // NZ, me % NZ
    way = 1 - 2 * (lax.axis_index("row") % 2)
    xs = (x + way * jnp.array(XPOS)) % NX
    zs = (z + way * jnp.array(ZPOS)) % NZ
    order = slab_order[(zs[:, None] + xs[None, :] * NZ).reshape(-1)]

    line = Line(jnp.zeros((8, T), jnp.float32))
    held = Held(blocks, amplitudes)
    flying = {}
    totals = []

    def land(axis, d):
        array, items = flying.pop((axis, d))
        held.put(line.hold(array), items)

    def send(axis, d, k, first=()):
        items = SENDS[axis, d][k]
        rows = lax.optimization_barrier((*first, held.rows(items)))[-1] if first else held.rows(items)
        if k:
            rows = line.hold(rows)
        moved = [(dx - d * (axis == "x"), dz - d * (axis == "z"), members) for dx, dz, members in items]
        flying[axis, d] = shift(rows, axis, d), moved

    def multiply():
        pieces, slabs = held.work()
        totals[:] = [line.hold(middle(blocks, pieces, slabs, high, low, totals, 10**9))]

    for d in (1, -1):
        for axis in "xz":
            send(axis, d, 0, () if d == 1 else (order,))
    for k in range(1, len(SENDS["x", 1])):
        for d in (1, -1):
            if k < 3:
                land("x", d)
                land("z", d)
                send("z", d, k)
            else:
                land("z", d)
                send("z", d, k)
                line.tick(10**9 if k == 3 else 10**9)
                land("x", d)
            send("x", d, k)
            if k > 1:
                multiply()
        if k == 1:
            order, integrals = line.hold(order, integrals)
            high, low = line.hold(*prepare(order, screen, integrals))
            multiply()
    for d in (1, -1):
        land("z", d)
        land("x", d)
        if d == 1:
            multiply()
    assert len(held.where) == 4 * NX * NZ
    pieces, slabs = held.work()
    ladder, energy = last(blocks, pieces, slabs, high, low, *totals, weights, line.token)
    for axis in ("row", "col"):
        size = lax.axis_size(axis)
        energy = lax.all_to_all(jnp.broadcast_to(energy, (size, 8, T)), axis, 0, 0).sum(axis=0)
    cells = count * lax.axis_size("row") * weights.shape[1] * lax.axis_size("col")
    return ladder, jnp.sum(energy) / cells


def solution(mesh):
    return jax.shard_map(
        local,
        mesh=mesh,
        in_specs=(P("row", "col"), P(None, "col"), P(None, "col"), P(), P("row", "col")),
        out_specs=(P("row", "col"), P()),
        check_vma=False,
    )
```

```python
import functools

import jax
import jax.numpy as jnp
from jax import lax
from jax.experimental import pallas as pl
from jax.experimental.pallas import tpu as pltpu
from jax.sharding import PartitionSpec as P

NX, NZ = 4, 8
XPOS = (0, -1, 1, 2)
ZPOS = (0, -1, 1, -2, 2, -3, 3, 4)
T = 128
MIB = 2**20
SLOTS = 16


def shift(v, axis, d):
    pairs = []
    for row in range(lax.axis_size("row")):
        step = d if row % 2 == 0 else -d
        for x in range(NX):
            for z in range(NZ):
                to = (x + step) % NX * NZ + z if axis == "x" else x * NZ + (z + step) % NZ
                pairs.append((row * NX * NZ + x * NZ + z, row * NX * NZ + to))
    return lax.ppermute(v, ("row", "col"), pairs)


def cost(flops):
    return pl.CostEstimate(flops=flops, bytes_accessed=0, transcendentals=0)


def tick_kernel(token_ref, out_ref):
    out_ref[...] = token_ref[...]


class Line:
    def __init__(self, token):
        self.token = token

    def tick(self, flops):
        self.token = pl.pallas_call(
            tick_kernel,
            out_shape=pltpu.VMEM(self.token.shape, self.token.dtype),
            in_specs=whole(1),
            out_specs=whole(1)[0],
            compiler_params=pltpu.CompilerParams(vmem_limit_bytes=MIB),
            cost_estimate=cost(flops),
            name="tick",
        )(*near((self.token,)))

    def hold(self, *values):
        self.token, *values = lax.optimization_barrier((self.token, *values))
        return values[0] if len(values) == 1 else values


def near(values):
    return [pltpu.with_memory_space_constraint(v, pltpu.VMEM) for v in values]


def whole(n):
    return [pl.BlockSpec(memory_space=pltpu.VMEM)] * n


def split(value):
    high = value.astype(jnp.bfloat16)
    return high, (value - high.astype(jnp.float32)).astype(jnp.bfloat16)


def pack_kernel(runs, *refs):
    out_ref, start = refs[-1], 0
    for i, first, end in runs:
        out_ref[pl.ds(start, end - first), :] = refs[i][pl.ds(first, end - first), :]
        start += end - first


def pack(runs):
    arrays = list({id(array): array for array, _, _ in runs}.values())
    places = {id(array): i for i, array in enumerate(arrays)}
    runs = [(places[id(array)], first, end) for array, first, end in runs]
    height = sum(end - first for _, first, end in runs)
    return pl.pallas_call(
        functools.partial(pack_kernel, runs),
        out_shape=pltpu.VMEM((height, T), jnp.float32),
        in_specs=whole(len(arrays)),
        out_specs=whole(1)[0],
        compiler_params=pltpu.CompilerParams(vmem_limit_bytes=MIB),
        cost_estimate=cost(1),
        name="pack",
    )(*near(arrays))


def prepare_kernel(order_ref, screen_ref, b_ref, high_ref, low_ref, slabs, arrived):
    slots, _, width = slabs.shape
    count = b_ref.shape[0] // T

    def copy(i):
        source = b_ref.at[pl.ds(pl.multiple_of(order_ref[i] * T, T), T), :]
        return pltpu.make_async_copy(source, slabs.at[i % slots], arrived.at[i % slots])

    @pl.loop(0, slots)
    def _(i):
        copy(i).start()

    @pl.loop(0, count)
    def _(i):
        copy(i).wait()
        rows = pl.ds(pl.multiple_of(i * T, T), T)
        for n in range(width // T):
            columns = pl.ds(n * T, T)
            kept = slabs[i % slots, :, columns] * screen_ref[order_ref[i], n].astype(jnp.float32)
            high_ref[rows, columns], low_ref[rows, columns] = split(kept)

        @pl.when(i + slots < count)
        def _():
            copy(i + slots).start()


def prepare(order, screen, integrals):
    depth, width = integrals.shape
    return pl.pallas_call(
        prepare_kernel,
        out_shape=[pltpu.VMEM((depth, width), jnp.bfloat16)] * 2,
        in_specs=[pl.BlockSpec(memory_space=pltpu.SMEM)] * 2 + [pl.BlockSpec(memory_space=pltpu.HBM)],
        out_specs=whole(2),
        scratch_shapes=[pltpu.VMEM((SLOTS, T, width), jnp.float32), pltpu.SemaphoreType.DMA((SLOTS,))],
        cost_estimate=cost(1),
        compiler_params=pltpu.CompilerParams(vmem_limit_bytes=6 * MIB),
        name="prepare",
    )(order, screen, pltpu.with_memory_space_constraint(integrals, pltpu.HBM))


def product(slabs, height, high_ref, low_ref):
    left = jnp.concatenate([piece[pl.ds(row, height), pl.ds(c * T, T)] for piece, row, c, place in slabs], axis=1)
    right = [jnp.concatenate([ref[pl.ds(s[3] * T, T), :] for s in slabs], axis=0) for ref in (high_ref, low_ref)]
    high, low = split(left)
    dot = functools.partial(jnp.dot, preferred_element_type=jnp.float32)
    two = dot(jnp.concatenate([high, low], axis=0), right[0])
    return two[:height] + (two[height:] + dot(high, right[1]))


def sums(blocks, work, pieces, high_ref, low_ref, emit):
    for (start, height), slabs in zip(blocks, work):
        slabs = [(pieces[i], row, c, place) for i, row, c, place in slabs]
        emit(start, height, product(slabs, height, high_ref, low_ref) if slabs else None)


def middle_kernel(blocks, work, n, first, *refs):
    pieces, (high_ref, low_ref), rest = refs[:n], refs[n : n + 2], refs[n + 2 :]
    total = rest[-1]

    def emit(start, height, value):
        rows = pl.ds(start, height)
        if value is not None:
            total[rows, :] = value if first else rest[0][rows, :] + value

    sums(blocks, work, pieces, high_ref, low_ref, emit)


def middle(blocks, pieces, work, high, low, totals, flops):
    width = high.shape[1]
    n = len(pieces)
    return pl.pallas_call(
        functools.partial(middle_kernel, blocks, work, n, not totals),
        out_shape=pltpu.VMEM((sum(height for _, height in blocks), width), jnp.float32),
        in_specs=whole(n + 2 + len(totals)),
        out_specs=whole(1)[0],
        input_output_aliases={n + 2 + i: i for i in range(len(totals))},
        compiler_params=pltpu.CompilerParams(vmem_limit_bytes=12 * MIB),
        cost_estimate=cost(flops),
        name="middle",
    )(*near((*pieces, high, low, *totals)))


def last_kernel(blocks, work, n, *refs):
    pieces, (high_ref, low_ref, total, weights_ref, zero_ref, ladder_ref, energy_ref) = refs[:n], refs[n:]
    energy_ref[...] = zero_ref[...]

    def emit(start, height, value):
        rows = pl.ds(start, height)
        value = 0.5 * (total[rows, :] if value is None else total[rows, :] + value)
        width = value.shape[1]
        ladder_ref[rows, :] = value
        terms = (weights_ref[rows, :] * value * value).reshape(height // 8, 8, width).sum(axis=0)
        energy_ref[...] += sum(terms[:, i * T : (i + 1) * T] for i in range(width // T))

    sums(blocks, work, pieces, high_ref, low_ref, emit)


def last(blocks, pieces, work, high, low, total, weights, zero):
    n = len(pieces)
    return pl.pallas_call(
        functools.partial(last_kernel, blocks, work, n),
        out_shape=[jax.ShapeDtypeStruct(weights.shape, jnp.float32), pltpu.VMEM((8, T), jnp.float32)],
        in_specs=whole(n + 5),
        out_specs=whole(2),
        compiler_params=pltpu.CompilerParams(vmem_limit_bytes=12 * MIB),
        name="last",
    )(*near((*pieces, high, low, total, weights, zero)))


ALL, INNER, OUTER, B0, B1, B2, B3 = (0, 1, 2, 3), (1, 2), (0, 3), (0,), (1,), (2,), (3,)
SENDS = {
    ("x", 1): (
        [(0, 0, ALL)],
        [(-1, 0, (0, 1)), (0, -1, INNER)],
        [(0, 1, INNER), (0, -2, INNER), (-1, -1, B1)],
        [(0, 2, INNER), (0, -3, INNER), (-1, 1, B1), (-1, -2, B1)],
        [(0, 3, INNER), (0, 4, B1), (-1, 2, B1), (-1, -3, B1)],
        [(0, 4, B2), (-1, 3, B1), (-1, 4, B1)],
    ),
    ("x", -1): (
        [(0, 0, ALL)],
        [(1, 0, (2, 3)), (0, -1, INNER), (0, 1, INNER)],
        [(0, -2, INNER), (0, 2, INNER), (1, -1, B2), (1, 1, B2)],
        [(0, -3, INNER), (0, 3, INNER), (1, -2, B2), (1, 2, B2)],
        [(0, 4, INNER), (1, -3, B2), (1, 3, B2)],
        [(1, 4, B2)],
    ),
    ("z", 1): (
        [(0, 0, ALL)],
        [(0, -1, ALL), (-1, 0, OUTER)],
        [(0, -2, ALL), (-1, -1, OUTER), (1, 0, OUTER), (2, 0, B0)],
        [(0, -3, (0, 1)), (-1, -2, OUTER), (1, -1, OUTER), (2, -1, B0), (2, 0, B3)],
        [(-1, -3, B0), (1, -2, OUTER), (2, -2, B0), (2, -1, B3)],
        [(1, -3, B0), (2, -3, B0), (2, -2, B3)],
    ),
    ("z", -1): (
        [(0, 0, ALL)],
        [(0, 1, ALL), (-1, 0, OUTER), (1, 0, OUTER)],
        [(0, 2, ALL), (-1, 1, OUTER), (1, 1, OUTER), (2, 0, OUTER)],
        [(0, 3, (2, 3)), (-1, 2, OUTER), (1, 2, OUTER), (2, 1, OUTER)],
        [(-1, 3, B3), (1, 3, B3), (2, 2, OUTER)],
        [(2, 3, B3)],
    ),
}


def wrap(value, size):
    return (value + size // 2 - 1) % size - size // 2 + 1


class Held:
    def __init__(self, blocks, own):
        self.blocks, self.where, self.fresh = blocks, {}, []
        self.put(own, [(0, 0, ALL)])

    def put(self, array, items):
        row = 0
        for dx, dz, members in items:
            for block in members:
                key = (wrap(dx, NX), wrap(dz, NZ), block)
                assert key not in self.where
                self.where[key] = (array, row)
                self.fresh.append(key)
                row += self.blocks[block][1]
        assert row == array.shape[0]

    def rows(self, items):
        runs = []
        for dx, dz, members in items:
            for block in members:
                array, row = self.where[dx, dz, block]
                height = self.blocks[block][1]
                if runs and runs[-1][0] is array and runs[-1][2] == row:
                    runs[-1][2] = row + height
                else:
                    runs.append([array, row, row + height])
        if len(runs) == 1:
            array, first, end = runs[0]
            return array if (first, end) == (0, array.shape[0]) else array[first:end]
        return pack(runs)

    def work(self):
        pieces, slabs = [], [[], [], [], []]
        for key in self.fresh:
            dx, dz, block = key
            array, row = self.where[key]
            number = [i for i, piece in enumerate(pieces) if piece is array]
            if not number:
                number = [len(pieces)]
                pieces.append(array)
            slabs[block].append((number[0], row, 0, ZPOS.index(dz) * NX + XPOS.index(dx)))
        self.fresh = []
        return pieces, slabs


def local(amplitudes, integrals, screen, slab_order, weights):
    count = amplitudes.shape[0]
    outer = count * 13 // 64
    inner = count // 2 - outer
    heights = (outer, inner, inner, outer)
    blocks = tuple((sum(heights[:i]), h) for i, h in enumerate(heights))
    me = lax.axis_index("col")
    x, z = me // NZ, me % NZ
    way = 1 - 2 * (lax.axis_index("row") % 2)
    xs = (x + way * jnp.array(XPOS)) % NX
    zs = (z + way * jnp.array(ZPOS)) % NZ
    order = slab_order[(zs[:, None] + xs[None, :] * NZ).reshape(-1)]

    line = Line(jnp.zeros((8, T), jnp.float32))
    held = Held(blocks, amplitudes)
    flying = {}
    totals = []

    def land(axis, d):
        array, items = flying.pop((axis, d))
        held.put(line.hold(array), items)

    def send(axis, d, k, first=()):
        items = SENDS[axis, d][k]
        rows = lax.optimization_barrier((*first, held.rows(items)))[-1] if first else held.rows(items)
        if k:
            rows = line.hold(rows)
        moved = [(dx - d * (axis == "x"), dz - d * (axis == "z"), members) for dx, dz, members in items]
        flying[axis, d] = shift(rows, axis, d), moved

    def multiply():
        pieces, slabs = held.work()
        totals[:] = [line.hold(middle(blocks, pieces, slabs, high, low, totals, 10**9))]

    for d in (1, -1):
        for axis in "xz":
            send(axis, d, 0, () if d == 1 else (order,))
    order, integrals = line.hold(order, integrals)
    high, low = line.hold(*prepare(order, screen, integrals))
    for k in range(1, len(SENDS["x", 1])):
        for d in (1, -1):
            if k < 3:
                land("x", d)
                land("z", d)
                send("z", d, k)
            else:
                land("z", d)
                send("z", d, k)
                line.tick(10**9 if k == 3 else 10**9)
                land("x", d)
            send("x", d, k)
            multiply()
    for d in (1, -1):
        land("z", d)
        land("x", d)
        if d == 1:
            multiply()
    assert len(held.where) == 4 * NX * NZ
    pieces, slabs = held.work()
    ladder, energy = last(blocks, pieces, slabs, high, low, *totals, weights, line.token)
    for axis in ("row", "col"):
        size = lax.axis_size(axis)
        energy = lax.all_to_all(jnp.broadcast_to(energy, (size, 8, T)), axis, 0, 0).sum(axis=0)
    cells = count * lax.axis_size("row") * weights.shape[1] * lax.axis_size("col")
    return ladder, jnp.sum(energy) / cells


def solution(mesh):
    return jax.shard_map(
        local,
        mesh=mesh,
        in_specs=(P("row", "col"), P(None, "col"), P(None, "col"), P(), P("row", "col")),
        out_specs=(P("row", "col"), P()),
        check_vma=False,
    )
```

```python
import functools

import jax
import jax.numpy as jnp
from jax import lax
from jax.experimental import pallas as pl
from jax.experimental.pallas import tpu as pltpu
from jax.sharding import PartitionSpec as P

NX, NZ = 4, 8
XPOS = (0, -1, 1, 2)
ZPOS = (0, -1, 1, -2, 2, -3, 3, 4)
T = 128
MIB = 2**20
SLOTS = 16


def shift(v, axis, d):
    pairs = []
    for x in range(NX):
        for z in range(NZ):
            to = (x + d) % NX * NZ + z if axis == "x" else x * NZ + (z + d) % NZ
            pairs.append((x * NZ + z, to))
    return lax.ppermute(v, "col", pairs)


def cost(flops):
    return pl.CostEstimate(flops=flops, bytes_accessed=0, transcendentals=0)


def tick_kernel(token_ref, out_ref):
    out_ref[...] = token_ref[...]


class Line:
    def __init__(self, token):
        self.token = token

    def tick(self, flops):
        self.token = pl.pallas_call(
            tick_kernel,
            out_shape=pltpu.VMEM(self.token.shape, self.token.dtype),
            in_specs=whole(1),
            out_specs=whole(1)[0],
            compiler_params=pltpu.CompilerParams(vmem_limit_bytes=MIB),
            cost_estimate=cost(flops),
            name="tick",
        )(*near((self.token,)))

    def hold(self, *values):
        self.token, *values = lax.optimization_barrier((self.token, *values))
        return values[0] if len(values) == 1 else values


def near(values):
    return [pltpu.with_memory_space_constraint(v, pltpu.VMEM) for v in values]


def whole(n):
    return [pl.BlockSpec(memory_space=pltpu.VMEM)] * n


def split(value):
    high = value.astype(jnp.bfloat16)
    return high, (value - high.astype(jnp.float32)).astype(jnp.bfloat16)


def pack_kernel(runs, *refs):
    out_ref, start = refs[-1], 0
    for i, first, end in runs:
        out_ref[pl.ds(start, end - first), :] = refs[i][pl.ds(first, end - first), :]
        start += end - first


def pack(runs):
    arrays = list({id(array): array for array, _, _ in runs}.values())
    places = {id(array): i for i, array in enumerate(arrays)}
    runs = [(places[id(array)], first, end) for array, first, end in runs]
    height = sum(end - first for _, first, end in runs)
    return pl.pallas_call(
        functools.partial(pack_kernel, runs),
        out_shape=pltpu.VMEM((height, T), jnp.float32),
        in_specs=whole(len(arrays)),
        out_specs=whole(1)[0],
        compiler_params=pltpu.CompilerParams(vmem_limit_bytes=MIB),
        cost_estimate=cost(1),
        name="pack",
    )(*near(arrays))


def prepare_kernel(order_ref, screen_ref, b_ref, high_ref, low_ref, slabs, arrived):
    slots, _, width = slabs.shape
    count = b_ref.shape[0] // T

    def copy(i):
        source = b_ref.at[pl.ds(pl.multiple_of(order_ref[i] * T, T), T), :]
        return pltpu.make_async_copy(source, slabs.at[i % slots], arrived.at[i % slots])

    @pl.loop(0, slots)
    def _(i):
        copy(i).start()

    @pl.loop(0, count)
    def _(i):
        copy(i).wait()
        rows = pl.ds(pl.multiple_of(i * T, T), T)
        for n in range(width // T):
            columns = pl.ds(n * T, T)
            kept = slabs[i % slots, :, columns] * screen_ref[order_ref[i], n].astype(jnp.float32)
            high_ref[rows, columns], low_ref[rows, columns] = split(kept)

        @pl.when(i + slots < count)
        def _():
            copy(i + slots).start()


def prepare(order, screen, integrals):
    depth, width = integrals.shape
    return pl.pallas_call(
        prepare_kernel,
        out_shape=[pltpu.VMEM((depth, width), jnp.bfloat16)] * 2,
        in_specs=[pl.BlockSpec(memory_space=pltpu.SMEM)] * 2 + [pl.BlockSpec(memory_space=pltpu.HBM)],
        out_specs=whole(2),
        scratch_shapes=[pltpu.VMEM((SLOTS, T, width), jnp.float32), pltpu.SemaphoreType.DMA((SLOTS,))],
        cost_estimate=cost(1),
        compiler_params=pltpu.CompilerParams(vmem_limit_bytes=6 * MIB),
        name="prepare",
    )(order, screen, pltpu.with_memory_space_constraint(integrals, pltpu.HBM))


def product(slabs, height, high_ref, low_ref):
    left = jnp.concatenate([piece[pl.ds(row, height), pl.ds(c * T, T)] for piece, row, c, place in slabs], axis=1)
    right = [jnp.concatenate([ref[pl.ds(s[3] * T, T), :] for s in slabs], axis=0) for ref in (high_ref, low_ref)]
    high, low = split(left)
    dot = functools.partial(jnp.dot, preferred_element_type=jnp.float32)
    two = dot(jnp.concatenate([high, low], axis=0), right[0])
    return two[:height] + (two[height:] + dot(high, right[1]))


def sums(blocks, work, pieces, high_ref, low_ref, emit):
    for (start, height), slabs in zip(blocks, work):
        slabs = [(pieces[i], row, c, place) for i, row, c, place in slabs]
        emit(start, height, product(slabs, height, high_ref, low_ref) if slabs else None)


def middle_kernel(blocks, work, n, first, *refs):
    pieces, (high_ref, low_ref), rest = refs[:n], refs[n : n + 2], refs[n + 2 :]
    total = rest[-1]

    def emit(start, height, value):
        rows = pl.ds(start, height)
        if value is not None:
            total[rows, :] = value if first else rest[0][rows, :] + value

    sums(blocks, work, pieces, high_ref, low_ref, emit)


def middle(blocks, pieces, work, high, low, totals, flops):
    width = high.shape[1]
    n = len(pieces)
    return pl.pallas_call(
        functools.partial(middle_kernel, blocks, work, n, not totals),
        out_shape=pltpu.VMEM((sum(height for _, height in blocks), width), jnp.float32),
        in_specs=whole(n + 2 + len(totals)),
        out_specs=whole(1)[0],
        input_output_aliases={n + 2 + i: i for i in range(len(totals))},
        compiler_params=pltpu.CompilerParams(vmem_limit_bytes=12 * MIB),
        cost_estimate=cost(flops),
        name="middle",
    )(*near((*pieces, high, low, *totals)))


def last_kernel(blocks, work, n, *refs):
    pieces, (high_ref, low_ref, total, weights_ref, zero_ref, ladder_ref, energy_ref) = refs[:n], refs[n:]
    energy_ref[...] = zero_ref[...]

    def emit(start, height, value):
        rows = pl.ds(start, height)
        value = 0.5 * (total[rows, :] if value is None else total[rows, :] + value)
        width = value.shape[1]
        ladder_ref[rows, :] = value
        terms = (weights_ref[rows, :] * value * value).reshape(height // 8, 8, width).sum(axis=0)
        energy_ref[...] += sum(terms[:, i * T : (i + 1) * T] for i in range(width // T))

    sums(blocks, work, pieces, high_ref, low_ref, emit)


def last(blocks, pieces, work, high, low, total, weights, zero):
    n = len(pieces)
    return pl.pallas_call(
        functools.partial(last_kernel, blocks, work, n),
        out_shape=[jax.ShapeDtypeStruct(weights.shape, jnp.float32), pltpu.VMEM((8, T), jnp.float32)],
        in_specs=whole(n + 5),
        out_specs=whole(2),
        compiler_params=pltpu.CompilerParams(vmem_limit_bytes=12 * MIB),
        name="last",
    )(*near((*pieces, high, low, total, weights, zero)))


ALL, INNER, OUTER, B0, B1, B2, B3 = (0, 1, 2, 3), (1, 2), (0, 3), (0,), (1,), (2,), (3,)
SENDS = {
    ("x", 1): (
        [(0, 0, ALL)],
        [(-1, 0, (0, 1)), (0, -1, INNER)],
        [(0, 1, INNER), (0, -2, INNER), (-1, -1, B1)],
        [(0, 2, INNER), (0, -3, INNER), (-1, 1, B1), (-1, -2, B1)],
        [(0, 3, INNER), (0, 4, B1), (-1, 2, B1), (-1, -3, B1)],
        [(0, 4, B2), (-1, 3, B1), (-1, 4, B1)],
    ),
    ("x", -1): (
        [(0, 0, ALL)],
        [(1, 0, (2, 3)), (0, -1, INNER), (0, 1, INNER)],
        [(0, -2, INNER), (0, 2, INNER), (1, -1, B2), (1, 1, B2)],
        [(0, -3, INNER), (0, 3, INNER), (1, -2, B2), (1, 2, B2)],
        [(0, 4, INNER), (1, -3, B2), (1, 3, B2)],
        [(1, 4, B2)],
    ),
    ("z", 1): (
        [(0, 0, ALL)],
        [(0, -1, ALL), (-1, 0, OUTER)],
        [(0, -2, ALL), (-1, -1, OUTER), (1, 0, OUTER), (2, 0, B0)],
        [(0, -3, (0, 1)), (-1, -2, OUTER), (1, -1, OUTER), (2, -1, B0), (2, 0, B3)],
        [(-1, -3, B0), (1, -2, OUTER), (2, -2, B0), (2, -1, B3)],
        [(1, -3, B0), (2, -3, B0), (2, -2, B3)],
    ),
    ("z", -1): (
        [(0, 0, ALL)],
        [(0, 1, ALL), (-1, 0, OUTER), (1, 0, OUTER)],
        [(0, 2, ALL), (-1, 1, OUTER), (1, 1, OUTER), (2, 0, OUTER)],
        [(0, 3, (2, 3)), (-1, 2, OUTER), (1, 2, OUTER), (2, 1, OUTER)],
        [(-1, 3, B3), (1, 3, B3), (2, 2, OUTER)],
        [(2, 3, B3)],
    ),
}


def wrap(value, size):
    return (value + size // 2 - 1) % size - size // 2 + 1


class Held:
    def __init__(self, blocks, own):
        self.blocks, self.where, self.fresh = blocks, {}, []
        self.put(own, [(0, 0, ALL)])

    def put(self, array, items):
        row = 0
        for dx, dz, members in items:
            for block in members:
                key = (wrap(dx, NX), wrap(dz, NZ), block)
                assert key not in self.where
                self.where[key] = (array, row)
                self.fresh.append(key)
                row += self.blocks[block][1]
        assert row == array.shape[0]

    def rows(self, items):
        runs = []
        for dx, dz, members in items:
            for block in members:
                array, row = self.where[dx, dz, block]
                height = self.blocks[block][1]
                if runs and runs[-1][0] is array and runs[-1][2] == row:
                    runs[-1][2] = row + height
                else:
                    runs.append([array, row, row + height])
        if len(runs) == 1:
            array, first, end = runs[0]
            return array if (first, end) == (0, array.shape[0]) else array[first:end]
        return pack(runs)

    def work(self):
        pieces, slabs = [], [[], [], [], []]
        for key in self.fresh:
            dx, dz, block = key
            array, row = self.where[key]
            number = [i for i, piece in enumerate(pieces) if piece is array]
            if not number:
                number = [len(pieces)]
                pieces.append(array)
            slabs[block].append((number[0], row, 0, ZPOS.index(dz) * NX + XPOS.index(dx)))
        self.fresh = []
        return pieces, slabs


def local(amplitudes, integrals, screen, slab_order, weights):
    count = amplitudes.shape[0]
    outer = count * 13 // 64
    inner = count // 2 - outer
    heights = (outer, inner, inner, outer)
    blocks = tuple((sum(heights[:i]), h) for i, h in enumerate(heights))
    me = lax.axis_index("col")
    x, z = me // NZ, me % NZ
    xs = (x + jnp.array(XPOS)) % NX
    zs = (z + jnp.array(ZPOS)) % NZ
    order = slab_order[(zs[:, None] + xs[None, :] * NZ).reshape(-1)]

    line = Line(jnp.zeros((8, T), jnp.float32))
    held = Held(blocks, amplitudes)
    flying = {}
    totals = []

    def land(axis, d):
        array, items = flying.pop((axis, d))
        held.put(line.hold(array), items)

    def send(axis, d, k, first=()):
        items = SENDS[axis, d][k]
        rows = lax.optimization_barrier((*first, held.rows(items)))[-1] if first else held.rows(items)
        if k:
            rows = line.hold(rows)
        moved = [(dx - d * (axis == "x"), dz - d * (axis == "z"), members) for dx, dz, members in items]
        flying[axis, d] = shift(rows, axis, d), moved

    def multiply():
        pieces, slabs = held.work()
        totals[:] = [line.hold(middle(blocks, pieces, slabs, high, low, totals, 10**9))]

    for d in (1, -1):
        for axis in "xz":
            send(axis, d, 0, () if d == 1 else (order,))
    order, integrals = line.hold(order, integrals)
    high, low = line.hold(*prepare(order, screen, integrals))
    for k in range(1, len(SENDS["x", 1])):
        for d in (1, -1):
            if k < 3:
                land("x", d)
                land("z", d)
                send("z", d, k)
            else:
                land("z", d)
                send("z", d, k)
                line.tick(10**9 if k == 3 else 10**9)
                land("x", d)
            send("x", d, k)
            multiply()
    for d in (1, -1):
        land("z", d)
        land("x", d)
        if d == 1:
            multiply()
    assert len(held.where) == 4 * NX * NZ
    pieces, slabs = held.work()
    ladder, energy = last(blocks, pieces, slabs, high, low, *totals, weights, line.token)
    for axis in ("row", "col"):
        size = lax.axis_size(axis)
        energy = lax.all_to_all(jnp.broadcast_to(energy, (size, 8, T)), axis, 0, 0).sum(axis=0)
    cells = count * lax.axis_size("row") * weights.shape[1] * lax.axis_size("col")
    return ladder, jnp.sum(energy) / cells


def solution(mesh):
    return jax.shard_map(
        local,
        mesh=mesh,
        in_specs=(P("row", "col"), P(None, "col"), P(None, "col"), P(), P("row", "col")),
        out_specs=(P("row", "col"), P()),
        check_vma=False,
    )
```

```python
import functools

import jax
import jax.numpy as jnp
from jax import lax
from jax.experimental import pallas as pl
from jax.experimental.pallas import tpu as pltpu
from jax.sharding import PartitionSpec as P

NX, NZ = 4, 8
XPOS = (0, -1, 1, 2)
ZPOS = (0, -1, 1, -2, 2, -3, 3, 4)
T = 128
MIB = 2**20
SLOTS = 16


def shift(v, axis, d):
    pairs = []
    for x in range(NX):
        for z in range(NZ):
            to = (x + d) % NX * NZ + z if axis == "x" else x * NZ + (z + d) % NZ
            pairs.append((x * NZ + z, to))
    return lax.ppermute(v, "col", pairs)


def cost(flops):
    return pl.CostEstimate(flops=flops, bytes_accessed=0, transcendentals=0)


def tick_kernel(token_ref, out_ref):
    out_ref[...] = token_ref[...]


class Line:
    def __init__(self, token):
        self.token = token

    def tick(self, flops):
        self.token = pl.pallas_call(
            tick_kernel,
            out_shape=pltpu.VMEM(self.token.shape, self.token.dtype),
            in_specs=whole(1),
            out_specs=whole(1)[0],
            compiler_params=pltpu.CompilerParams(vmem_limit_bytes=MIB),
            cost_estimate=cost(flops),
            name="tick",
        )(*near((self.token,)))

    def hold(self, *values):
        self.token, *values = lax.optimization_barrier((self.token, *values))
        return values[0] if len(values) == 1 else values


def near(values):
    return [pltpu.with_memory_space_constraint(v, pltpu.VMEM) for v in values]


def whole(n):
    return [pl.BlockSpec(memory_space=pltpu.VMEM)] * n


def split(value):
    high = value.astype(jnp.bfloat16)
    return high, (value - high.astype(jnp.float32)).astype(jnp.bfloat16)


def pack_kernel(runs, *refs):
    out_ref, start = refs[-1], 0
    for i, first, end in runs:
        out_ref[pl.ds(start, end - first), :] = refs[i][pl.ds(first, end - first), :]
        start += end - first


def pack(runs):
    arrays = list({id(array): array for array, _, _ in runs}.values())
    places = {id(array): i for i, array in enumerate(arrays)}
    runs = [(places[id(array)], first, end) for array, first, end in runs]
    height = sum(end - first for _, first, end in runs)
    return pl.pallas_call(
        functools.partial(pack_kernel, runs),
        out_shape=pltpu.VMEM((height, T), jnp.float32),
        in_specs=whole(len(arrays)),
        out_specs=whole(1)[0],
        compiler_params=pltpu.CompilerParams(vmem_limit_bytes=MIB),
        cost_estimate=cost(1),
        name="pack",
    )(*near(arrays))


def prepare_kernel(order_ref, screen_ref, b_ref, high_ref, low_ref, slabs, arrived):
    slots, _, width = slabs.shape
    count = b_ref.shape[0] // T

    def copy(i):
        source = b_ref.at[pl.ds(pl.multiple_of(order_ref[i] * T, T), T), :]
        return pltpu.make_async_copy(source, slabs.at[i % slots], arrived.at[i % slots])

    @pl.loop(0, slots)
    def _(i):
        copy(i).start()

    @pl.loop(0, count)
    def _(i):
        copy(i).wait()
        rows = pl.ds(pl.multiple_of(i * T, T), T)
        for n in range(width // T):
            columns = pl.ds(n * T, T)
            kept = slabs[i % slots, :, columns] * screen_ref[order_ref[i], n].astype(jnp.float32)
            high_ref[rows, columns], low_ref[rows, columns] = split(kept)

        @pl.when(i + slots < count)
        def _():
            copy(i + slots).start()


def prepare(order, screen, integrals):
    depth, width = integrals.shape
    return pl.pallas_call(
        prepare_kernel,
        out_shape=[pltpu.VMEM((depth, width), jnp.bfloat16)] * 2,
        in_specs=[pl.BlockSpec(memory_space=pltpu.SMEM)] * 2 + [pl.BlockSpec(memory_space=pltpu.HBM)],
        out_specs=whole(2),
        scratch_shapes=[pltpu.VMEM((SLOTS, T, width), jnp.float32), pltpu.SemaphoreType.DMA((SLOTS,))],
        cost_estimate=cost(1),
        compiler_params=pltpu.CompilerParams(vmem_limit_bytes=6 * MIB),
        name="prepare",
    )(order, screen, pltpu.with_memory_space_constraint(integrals, pltpu.HBM))


def product(slabs, height, high_ref, low_ref):
    left = jnp.concatenate([piece[pl.ds(row, height), pl.ds(c * T, T)] for piece, row, c, place in slabs], axis=1)
    right = [jnp.concatenate([ref[pl.ds(s[3] * T, T), :] for s in slabs], axis=0) for ref in (high_ref, low_ref)]
    high, low = split(left)
    dot = functools.partial(jnp.dot, preferred_element_type=jnp.float32)
    two = dot(jnp.concatenate([high, low], axis=0), right[0])
    return two[:height] + (two[height:] + dot(high, right[1]))


def sums(blocks, work, pieces, high_ref, low_ref, emit):
    for (start, height), slabs in zip(blocks, work):
        slabs = [(pieces[i], row, c, place) for i, row, c, place in slabs]
        emit(start, height, product(slabs, height, high_ref, low_ref) if slabs else None)


def middle_kernel(blocks, work, n, first, *refs):
    pieces, (high_ref, low_ref), rest = refs[:n], refs[n : n + 2], refs[n + 2 :]
    total = rest[-1]

    def emit(start, height, value):
        rows = pl.ds(start, height)
        if value is not None:
            total[rows, :] = value if first else rest[0][rows, :] + value

    sums(blocks, work, pieces, high_ref, low_ref, emit)


def middle(blocks, pieces, work, high, low, totals, flops):
    width = high.shape[1]
    n = len(pieces)
    return pl.pallas_call(
        functools.partial(middle_kernel, blocks, work, n, not totals),
        out_shape=pltpu.VMEM((sum(height for _, height in blocks), width), jnp.float32),
        in_specs=whole(n + 2 + len(totals)),
        out_specs=whole(1)[0],
        input_output_aliases={n + 2 + i: i for i in range(len(totals))},
        compiler_params=pltpu.CompilerParams(vmem_limit_bytes=12 * MIB),
        cost_estimate=cost(flops),
        name="middle",
    )(*near((*pieces, high, low, *totals)))


def last_kernel(blocks, work, n, *refs):
    pieces, (high_ref, low_ref, total, weights_ref, zero_ref, ladder_ref, energy_ref) = refs[:n], refs[n:]
    energy_ref[...] = zero_ref[...]

    def emit(start, height, value):
        rows = pl.ds(start, height)
        value = 0.5 * (total[rows, :] if value is None else total[rows, :] + value)
        width = value.shape[1]
        ladder_ref[rows, :] = value
        terms = (weights_ref[rows, :] * value * value).reshape(height // 8, 8, width).sum(axis=0)
        energy_ref[...] += sum(terms[:, i * T : (i + 1) * T] for i in range(width // T))

    sums(blocks, work, pieces, high_ref, low_ref, emit)


def last(blocks, pieces, work, high, low, total, weights, zero):
    n = len(pieces)
    return pl.pallas_call(
        functools.partial(last_kernel, blocks, work, n),
        out_shape=[jax.ShapeDtypeStruct(weights.shape, jnp.float32), pltpu.VMEM((8, T), jnp.float32)],
        in_specs=whole(n + 5),
        out_specs=whole(2),
        compiler_params=pltpu.CompilerParams(vmem_limit_bytes=12 * MIB),
        name="last",
    )(*near((*pieces, high, low, total, weights, zero)))


ALL, INNER, OUTER, B0, B1, B2, B3 = (0, 1, 2, 3), (1, 2), (0, 3), (0,), (1,), (2,), (3,)
SENDS = {
    ("x", 1): (
        [(0, 0, ALL)],
        [(-1, 0, (0, 1)), (0, -1, INNER)],
        [(0, 1, INNER), (0, -2, INNER), (-1, -1, B1)],
        [(0, 2, INNER), (0, -3, INNER), (-1, 1, B1), (-1, -2, B1)],
        [(0, 3, INNER), (0, 4, B1), (-1, 2, B1), (-1, -3, B1)],
        [(0, 4, B2), (-1, 3, B1), (-1, 4, B1)],
    ),
    ("x", -1): (
        [(0, 0, ALL)],
        [(1, 0, (2, 3)), (0, -1, INNER), (0, 1, INNER)],
        [(0, -2, INNER), (0, 2, INNER), (1, -1, B2), (1, 1, B2)],
        [(0, -3, INNER), (0, 3, INNER), (1, -2, B2), (1, 2, B2)],
        [(0, 4, INNER), (1, -3, B2), (1, 3, B2)],
        [(1, 4, B2)],
    ),
    ("z", 1): (
        [(0, 0, ALL)],
        [(0, -1, ALL), (-1, 0, OUTER)],
        [(0, -2, ALL), (-1, -1, OUTER), (1, 0, OUTER), (2, 0, B0)],
        [(0, -3, (0, 1)), (-1, -2, OUTER), (1, -1, OUTER), (2, -1, B0), (2, 0, B3)],
        [(-1, -3, B0), (1, -2, OUTER), (2, -2, B0), (2, -1, B3)],
        [(1, -3, B0), (2, -3, B0), (2, -2, B3)],
    ),
    ("z", -1): (
        [(0, 0, ALL)],
        [(0, 1, ALL), (-1, 0, OUTER), (1, 0, OUTER)],
        [(0, 2, ALL), (-1, 1, OUTER), (1, 1, OUTER), (2, 0, OUTER)],
        [(0, 3, (2, 3)), (-1, 2, OUTER), (1, 2, OUTER), (2, 1, OUTER)],
        [(-1, 3, B3), (1, 3, B3), (2, 2, OUTER)],
        [(2, 3, B3)],
    ),
}


def wrap(value, size):
    return (value + size // 2 - 1) % size - size // 2 + 1


class Held:
    def __init__(self, blocks, own):
        self.blocks, self.where, self.fresh = blocks, {}, []
        self.put(own, [(0, 0, ALL)])

    def put(self, array, items):
        row = 0
        for dx, dz, members in items:
            for block in members:
                key = (wrap(dx, NX), wrap(dz, NZ), block)
                assert key not in self.where
                self.where[key] = (array, row)
                self.fresh.append(key)
                row += self.blocks[block][1]
        assert row == array.shape[0]

    def rows(self, items):
        runs = []
        for dx, dz, members in items:
            for block in members:
                array, row = self.where[dx, dz, block]
                height = self.blocks[block][1]
                if runs and runs[-1][0] is array and runs[-1][2] == row:
                    runs[-1][2] = row + height
                else:
                    runs.append([array, row, row + height])
        if len(runs) == 1:
            array, first, end = runs[0]
            return array if (first, end) == (0, array.shape[0]) else array[first:end]
        return pack(runs)

    def work(self):
        pieces, slabs = [], [[], [], [], []]
        for key in self.fresh:
            dx, dz, block = key
            array, row = self.where[key]
            number = [i for i, piece in enumerate(pieces) if piece is array]
            if not number:
                number = [len(pieces)]
                pieces.append(array)
            slabs[block].append((number[0], row, 0, ZPOS.index(dz) * NX + XPOS.index(dx)))
        self.fresh = []
        return pieces, slabs


def local(amplitudes, integrals, screen, slab_order, weights):
    count = amplitudes.shape[0]
    outer = count * 12 // 64
    inner = count // 2 - outer
    heights = (outer, inner, inner, outer)
    blocks = tuple((sum(heights[:i]), h) for i, h in enumerate(heights))
    me = lax.axis_index("col")
    x, z = me // NZ, me % NZ
    xs = (x + jnp.array(XPOS)) % NX
    zs = (z + jnp.array(ZPOS)) % NZ
    order = slab_order[(zs[:, None] + xs[None, :] * NZ).reshape(-1)]

    line = Line(jnp.zeros((8, T), jnp.float32))
    held = Held(blocks, amplitudes)
    flying = {}
    totals = []

    def land(axis, d):
        array, items = flying.pop((axis, d))
        held.put(line.hold(array), items)

    def send(axis, d, k, first=()):
        items = SENDS[axis, d][k]
        rows = lax.optimization_barrier((*first, held.rows(items)))[-1] if first else held.rows(items)
        if k:
            rows = line.hold(rows)
        moved = [(dx - d * (axis == "x"), dz - d * (axis == "z"), members) for dx, dz, members in items]
        flying[axis, d] = shift(rows, axis, d), moved

    def multiply():
        pieces, slabs = held.work()
        totals[:] = [line.hold(middle(blocks, pieces, slabs, high, low, totals, 10**9))]

    for d in (1, -1):
        for axis in "xz":
            send(axis, d, 0)
    order, integrals = line.hold(order, integrals)
    high, low = line.hold(*prepare(order, screen, integrals))
    for k in range(1, len(SENDS["x", 1])):
        for d in (1, -1):
            if k < 3:
                land("x", d)
                land("z", d)
                send("z", d, k)
            else:
                land("z", d)
                send("z", d, k)
                line.tick(10**9 if k == 3 else 10**9)
                land("x", d)
            send("x", d, k)
            multiply()
    for d in (1, -1):
        land("z", d)
        land("x", d)
        if d == 1:
            multiply()
    assert len(held.where) == 4 * NX * NZ
    pieces, slabs = held.work()
    ladder, energy = last(blocks, pieces, slabs, high, low, *totals, weights, line.token)
    for axis in ("row", "col"):
        size = lax.axis_size(axis)
        energy = lax.all_to_all(jnp.broadcast_to(energy, (size, 8, T)), axis, 0, 0).sum(axis=0)
    cells = count * lax.axis_size("row") * weights.shape[1] * lax.axis_size("col")
    return ladder, jnp.sum(energy) / cells


def solution(mesh):
    return jax.shard_map(
        local,
        mesh=mesh,
        in_specs=(P("row", "col"), P(None, "col"), P(None, "col"), P(), P("row", "col")),
        out_specs=(P("row", "col"), P()),
        check_vma=False,
    )
```
